128 devices in a mesh: row: 16 (over x, y_lo, core), col: 8 (over y_hi, z).
Axes of the slice: x: 4, y: 4 (y_hi: 2, y_lo: 2; y = y_hi * 2 + y_lo), z: 4, core: 2. Of those that a mesh axis runs over, the one named last changes fastest.
Arguments:
- embeddings: bfloat16 [16384, 1024], P(('row', 'col'))
- partner: int32 [16384], P(('row', 'col')), may hold values from 0 to 16383, as said below
- inv_temp: float32 [1], replicated, may hold values from 8 to 128
Outputs:
- loss: float32 [1], replicated
- grad_embed: float32 [16384, 1024], P(('row', 'col'))
The draws below stay inside these ranges and needn't reach their ends.
Inputs may be any that keep to these rules, and one draw needn't show every extreme that they name: partner pairs the views: partner[partner[i]] == i and partner[i] != i for every view.
All inputs are finite; a program needn't handle non-finite values.
Results may differ from the reference program's by a relative error of at most 0.0065.
The reference program's roundings to bfloat16 on the way (of `unit_b` and `coef`) count: a program that leaves them out, or rounds other values in their place, can miss the bound.
Values may be sent and summed in bfloat16 or wider, within the bound.
No kernel may reach another device: no remote copies, remote signals or barrier semaphores. Data moves between devices by JAX's collectives and lax.ppermute only.
A program may use at most 64 MiB of HBM per device.

```python
import math
import jax
import jax.numpy as jnp
from jax import lax

PROJ = 1024
VIEWS = 16384


def pair_order(key):
    return jax.random.permutation(jax.random.fold_in(key, 5), VIEWS).astype(jnp.int32)


def draw_partner(key, part):
    order = pair_order(key)
    first = order[0::2]
    second = order[1::2]
    mates = jnp.zeros((VIEWS,), jnp.int32)
    mates = mates.at[first].set(second)
    mates = mates.at[second].set(first)
    return mates


def draw_embeddings(key, part):
    order = pair_order(key)
    key = jax.random.fold_in(key, 11)
    pair_of = jnp.zeros((VIEWS,), jnp.int32).at[order].set(jnp.arange(VIEWS, dtype=jnp.int32) // 2)
    shared = jax.random.normal(jax.random.fold_in(key, 1), (VIEWS // 2, PROJ), jnp.float32)
    noise = jax.random.normal(jax.random.fold_in(key, 2), (VIEWS, PROJ), jnp.float32)
    values = shared[pair_of] + 0.75 * noise
    return values.astype(jnp.bfloat16)


def draw_inv_temp(key, part):
    key = jax.random.fold_in(key, 13)
    values = jnp.exp(jax.random.uniform(key, (1,), jnp.float32, 2.0794, 4.852))
    return values.astype(jnp.float32)


def setup_inputs(seed: int = 0) -> dict:
    key_of = jax.random.split(jax.random.key(seed), 4)
    return {
        "embeddings": draw_embeddings(jax.random.fold_in(key_of[3], 71), 0),
        "partner": draw_partner(jax.random.fold_in(key_of[3], 71), 0),
        "inv_temp": draw_inv_temp(jax.random.fold_in(key_of[3], 71), 0),
    }


def normalize(embeddings):
    flat = embeddings.astype(jnp.float32)
    inv_norm = lax.rsqrt(lax.optimization_barrier(jnp.sum(flat * flat, axis=1, keepdims=True)) + 1e-06)
    return (flat * inv_norm, inv_norm)

def reference(embeddings, partner, inv_temp):
    unit, inv_norm = normalize(embeddings)
    unit_b = unit.astype(jnp.bfloat16)
    scale = inv_temp[0]
    block = math.gcd(VIEWS, 512)
    count = VIEWS // block
    columns = jnp.arange(VIEWS, dtype=jnp.int32)

    def scores_of(start):
        rows = lax.dynamic_slice_in_dim(unit_b, start, block, 0)
        scores = scale * jnp.dot(rows, unit_b.T, preferred_element_type=jnp.float32)
        index = start + jnp.arange(block, dtype=jnp.int32)
        scores = jnp.where(index[:, None] == columns[None, :], -jnp.inf, scores)
        mates = lax.dynamic_slice_in_dim(partner, start, block, 0)
        return (rows, scores, mates)

    def forward(number):
        rows, scores, mates = scores_of(number * block)
        peak = lax.optimization_barrier(jnp.max(scores, axis=1))
        lse = peak + jnp.log(lax.optimization_barrier(jnp.sum(jnp.exp(scores - peak[:, None]), axis=1)))
        pos = lax.optimization_barrier(jnp.sum(jnp.where(columns[None, :] == mates[:, None], scores, 0.0), axis=1))
        return (lse, pos)
    numbers = jnp.arange(count, dtype=jnp.int32)
    lse, pos = lax.map(forward, numbers)
    lse = lse.reshape(-1)
    pos = pos.reshape(-1)
    loss = jnp.mean(lse - pos).reshape(1)

    def backward(dunit, number):
        start = number * block
        rows, scores, mates = scores_of(start)
        lse_rows = lax.dynamic_slice_in_dim(lse, start, block, 0)
        prob = jnp.exp(scores - lse_rows[:, None])
        target = jnp.where(columns[None, :] == mates[:, None], 1.0, 0.0)
        coef = ((prob - target) / VIEWS).astype(jnp.bfloat16)
        row_part = jnp.dot(coef, unit_b, preferred_element_type=jnp.float32)
        col_part = jnp.dot(coef.T, rows, preferred_element_type=jnp.float32)
        dunit = dunit + col_part
        current = lax.dynamic_slice_in_dim(dunit, start, block, 0)
        dunit = lax.dynamic_update_slice_in_dim(dunit, current + row_part, start, 0)
        return (dunit, None)
    dunit, _ = lax.scan(backward, jnp.zeros((VIEWS, PROJ), jnp.float32), numbers)
    dunit = scale * dunit
    grad_embed = inv_norm * (dunit - unit * lax.optimization_barrier(jnp.sum(unit * dunit, axis=1, keepdims=True)))
    return (loss, grad_embed)
```

```python
import functools
import numpy as np
import jax
import jax.numpy as jnp
from jax import lax
from jax.experimental import pallas as pl
from jax.experimental.pallas import tpu as pltpu
from jax.sharding import PartitionSpec as P

LOG2E = 1.4426950408889634
LN2 = 0.6931471805599453
F32 = jnp.float32
BF16 = jnp.bfloat16


def device_id(x, y, z, core):
    return ((x % 4) * 4 + (y % 2) * 2 + core) * 8 + (y % 4) // 2 * 4 + z % 4


def groups_of_rows():
    return [
        [device_id(x, y, z, k) for y in (p, p + 1) for z in range(4)]
        for x in range(4)
        for p in (0, 2)
        for k in range(2)
    ]


def groups_of_columns():
    return [
        [device_id(x, y, z, k) for y in (p, p + 1) for x in range(4)]
        for z in range(4)
        for p in (1, 3)
        for k in range(2)
    ]


def table(groups):
    rows = np.zeros((128, len(groups[0])), np.int32)
    for g in groups:
        for d in g:
            rows[d] = g
    return rows


def unit_kernel(x_ref, out_ref):
    flat = x_ref[...].astype(F32)
    inv = lax.rsqrt(jnp.sum(flat * flat, axis=1, keepdims=True) + 1e-06)
    out_ref[...] = (flat * inv).astype(BF16)


def score_kernel(scale_ref, a_ref, b_ref, rows_ref, mates_ref, cols_ref, s_ref, peak_ref, sums_ref, pos_ref):
    scale2 = scale_ref[0] * LOG2E
    s = lax.dot_general(a_ref[...], b_ref[...], (((1,), (1,)), ((), ())), preferred_element_type=F32)
    s = s * scale2
    cols = cols_ref[...]
    s = jnp.where(rows_ref[...] == cols, -jnp.inf, s)
    s_ref[...] = s
    peak = jnp.max(s, axis=1, keepdims=True)
    peak_ref[...] = peak
    sums_ref[...] = jnp.sum(jnp.exp2(s - peak), axis=1, keepdims=True)
    pos_ref[...] = jnp.sum(jnp.where(mates_ref[...] == cols, s, 0.0), axis=1, keepdims=True)


def grad_kernel(s_ref, b_ref, lse_row_ref, lse_col_ref, mates_ref, cols_ref, out_ref):
    s = s_ref[...]
    d = jnp.exp2(s - lse_row_ref[...]) + jnp.exp2(s - lse_col_ref[...])
    d = d - jnp.where(mates_ref[...] == cols_ref[...], 2.0, 0.0)
    out_ref[...] = jnp.dot(d.astype(BF16), b_ref[...], preferred_element_type=F32).astype(BF16)


def final_kernel(scale_ref, x_ref, parts_ref, out_ref):
    flat = x_ref[...].astype(F32)
    inv = lax.rsqrt(jnp.sum(flat * flat, axis=1, keepdims=True) + 1e-06)
    unit = flat * inv
    dunit = jnp.sum(parts_ref[...].astype(F32), axis=0) * (scale_ref[0] / 16384.0)
    out_ref[...] = inv * (dunit - unit * jnp.sum(unit * dunit, axis=1, keepdims=True))


VMEM = pl.BlockSpec(memory_space=pltpu.VMEM)
SMEM = pl.BlockSpec(memory_space=pltpu.SMEM)


def body(embeddings, partner, inv_temp):
    views, width = embeddings.shape
    me = lax.axis_index("row") * 8 + lax.axis_index("col")
    rows_groups, cols_groups = groups_of_rows(), groups_of_columns()
    other_core = [(d, d ^ 8) for d in range(128)]
    axes = ("row", "col")

    def spread(v, groups):
        n = len(groups[0])
        v = jnp.broadcast_to(v[None], (n, *v.shape))
        return lax.all_to_all(v, axes, 0, 0, tiled=True, axis_index_groups=groups)

    unit_b = pl.pallas_call(
        unit_kernel, out_shape=jax.ShapeDtypeStruct((views, width), BF16), in_specs=[VMEM], out_specs=VMEM
    )(embeddings)
    mates = spread(partner.reshape(1, views), rows_groups).reshape(-1, 1)
    block_a = spread(unit_b, rows_groups).reshape(-1, width)
    block_b = spread(unit_b, cols_groups).reshape(-1, width)
    block_b2 = lax.ppermute(block_b, axes, other_core)
    block_b = jnp.concatenate([block_b, block_b2], axis=0)
    n_a, n_b = block_a.shape[0], block_b.shape[0]
    ids_a = jnp.asarray(table(rows_groups))[me]
    ids_b = jnp.asarray(table(cols_groups))[me]
    ids_b = jnp.concatenate([ids_b, ids_b ^ 8])
    lane = jnp.arange(views, dtype=jnp.int32)
    rows_global = (ids_a[:, None] * views + lane[None, :]).reshape(n_a, 1)
    cols_global = (ids_b[:, None] * views + lane[None, :]).reshape(1, n_b)

    bm = 256
    col_spec = pl.BlockSpec((bm, 1), lambda i: (i, 0))
    scores, peak, sums, pos = pl.pallas_call(
        score_kernel,
        grid=(n_a // bm,),
        out_shape=[
            jax.ShapeDtypeStruct((n_a, n_b), F32),
            jax.ShapeDtypeStruct((n_a, 1), F32),
            jax.ShapeDtypeStruct((n_a, 1), F32),
            jax.ShapeDtypeStruct((n_a, 1), F32),
        ],
        in_specs=[
            SMEM,
            pl.BlockSpec((bm, width), lambda i: (i, 0)),
            pl.BlockSpec((n_b, width), lambda i: (0, 0)),
            col_spec,
            col_spec,
            pl.BlockSpec((1, n_b), lambda i: (0, 0)),
        ],
        out_specs=[pl.BlockSpec((bm, n_b), lambda i: (i, 0)), col_spec, col_spec, col_spec],
        compiler_params=pltpu.CompilerParams(vmem_limit_bytes=48 << 20),
    )(inv_temp, block_a, block_b, rows_global, mates, cols_global)

    stats = jnp.concatenate([peak.reshape(8, views), sums.reshape(8, views), pos.reshape(8, views)], axis=0)
    stats = spread(stats, rows_groups).reshape(8, 3, 8, views)
    peak_all = jnp.max(stats[:, 0], axis=0)
    lse2 = peak_all + jnp.log2(jnp.sum(stats[:, 1] * jnp.exp2(stats[:, 0] - peak_all), axis=0))
    loss_rows = jnp.sum(lse2) - jnp.sum(stats[:, 2])
    position = jnp.argmax(ids_a == me)
    own_lse = lax.dynamic_slice_in_dim(lse2, position, 1, 0)
    payload = jnp.concatenate([own_lse, jnp.full((1, views), loss_rows)], axis=0)
    gathered = spread(payload, cols_groups).reshape(8, 2, views)
    swapped = lax.ppermute(gathered, axes, other_core)
    gathered = jnp.concatenate([gathered, swapped], axis=0)
    loss = (jnp.sum(gathered[:, 1, 0]) * (LN2 / 16384.0)).reshape(1)
    lse_cols = gathered[:, 0].reshape(1, n_b)

    grads = pl.pallas_call(
        grad_kernel,
        grid=(n_a // bm,),
        out_shape=jax.ShapeDtypeStruct((n_a, width), BF16),
        in_specs=[
            pl.BlockSpec((bm, n_b), lambda i: (i, 0)),
            pl.BlockSpec((n_b, width), lambda i: (0, 0)),
            col_spec,
            pl.BlockSpec((1, n_b), lambda i: (0, 0)),
            col_spec,
            pl.BlockSpec((1, n_b), lambda i: (0, 0)),
        ],
        out_specs=pl.BlockSpec((bm, width), lambda i: (i, 0)),
        compiler_params=pltpu.CompilerParams(vmem_limit_bytes=48 << 20),
    )(scores, block_b, lse2.reshape(n_a, 1), lse_cols, mates, cols_global)
    parts = lax.all_to_all(grads.reshape(8, views, width), axes, 0, 0, tiled=True, axis_index_groups=rows_groups)
    grad_embed = pl.pallas_call(
        final_kernel,
        out_shape=jax.ShapeDtypeStruct((views, width), F32),
        in_specs=[SMEM, VMEM, VMEM],
        out_specs=VMEM,
    )(inv_temp, embeddings, parts)
    return loss, grad_embed


def solution(mesh):
    in_specs = (P(("row", "col"), None), P(("row", "col")), P())
    out_specs = (P(), P(("row", "col"), None))
    return jax.shard_map(body, mesh=mesh, in_specs=in_specs, out_specs=out_specs, check_vma=False)
```

```python
import functools

import jax
import jax.numpy as jnp
from jax import lax
from jax.experimental import pallas as pl
from jax.experimental.pallas import tpu as pltpu
from jax.sharding import PartitionSpec as P

F32 = jnp.float32
BF16 = jnp.bfloat16
BLOCK = 256
VMEM = pl.BlockSpec(memory_space=pltpu.VMEM)
SMEM = pl.BlockSpec(memory_space=pltpu.SMEM)


def eye(n):
    return lax.broadcasted_iota(jnp.int32, (n, n), 0) == lax.broadcasted_iota(jnp.int32, (n, n), 1)


def to_column(row):
    n = row.shape[1]
    return jnp.sum(jnp.where(eye(n), row, jnp.zeros_like(row)), axis=1, keepdims=True)


def to_row(column):
    n = column.shape[0]
    return jnp.sum(jnp.where(eye(n), column, jnp.zeros_like(column)), axis=0, keepdims=True)


def unit_kernel(x_ref, out_ref, copies_ref):
    flat = x_ref[...].astype(F32)
    inv = lax.rsqrt(jnp.sum(flat * flat, axis=1, keepdims=True) + 1e-06)
    unit_b = (flat * inv).astype(BF16)
    out_ref[...] = unit_b
    for i in range(copies_ref.shape[0]):
        copies_ref[i] = unit_b


def columns_of(mates_ref, start, shards):
    return jnp.concatenate([to_column(mates_ref[pl.ds(start + i, 1), :]) for i in range(shards)], axis=0)


def score_kernel(place_ref, scale_ref, a_ref, b_ref, mates_ref, s_ref, stats_ref):
    step = pl.program_id(0)
    row_pos, col_pos = place_ref[0], place_ref[1]
    scale = scale_ref[0]
    a = a_ref[...]
    n_b, lanes = b_ref.shape[0], 128
    wide = 512
    for j in range(n_b // wide):
        part = lax.dot_general(
            a, b_ref[j * wide : (j + 1) * wide, :], (((1,), (1,)), ((), ())), preferred_element_type=F32
        )
        s_ref[:, j * wide : (j + 1) * wide] = part * scale
    per = BLOCK // lanes

    @pl.when(col_pos // per == step)
    def _():
        rows = pl.ds(pl.multiple_of(col_pos % per * lanes, lanes), lanes)
        cols = pl.ds(pl.multiple_of(row_pos * lanes, lanes), lanes)
        s_ref[rows, cols] = jnp.where(eye(lanes), -jnp.inf, s_ref[rows, cols])

    for i in range(per):
        rows = slice(i * lanes, (i + 1) * lanes)
        mates = to_column(mates_ref[pl.ds(step * per + i, 1), :])
        lane = lax.broadcasted_iota(jnp.int32, (lanes, lanes), 1)
        peak = s_ref[rows, 0:lanes]
        for t in range(1, n_b // lanes):
            peak = jnp.maximum(peak, s_ref[rows, t * lanes : (t + 1) * lanes])
        peak = jnp.max(peak, axis=1, keepdims=True)
        sums = jnp.zeros((lanes, lanes), F32)
        pos = jnp.zeros((lanes, lanes), F32)
        for t in range(n_b // lanes):
            s = s_ref[rows, t * lanes : (t + 1) * lanes]
            sums = sums + jnp.exp(s - peak)
            pos = pos + jnp.where(lane == mates - t * lanes, s, 0.0)
        shard = step * per + i
        peak, sums, pos = (to_row(v) for v in (peak, jnp.sum(sums, axis=1, keepdims=True), jnp.sum(pos, axis=1, keepdims=True)))
        for dest in range(stats_ref.shape[0]):
            stats_ref[dest, 0, pl.ds(shard, 1), :] = peak
            stats_ref[dest, 1, pl.ds(shard, 1), :] = sums
            stats_ref[dest, 2, pl.ds(shard, 1), :] = pos


def merge_kernel(place_ref, stats_ref, lse_ref, out_ref):
    peak = jnp.max(stats_ref[:, 0], axis=0)
    total = jnp.zeros_like(peak)
    pos = jnp.zeros_like(peak)
    for i in range(stats_ref.shape[0]):
        total = total + stats_ref[i, 1] * jnp.exp(stats_ref[i, 0] - peak)
        pos = pos + stats_ref[i, 2]
    lse = peak + jnp.log(total)
    lse_ref[...] = lse
    shard = lax.broadcasted_iota(jnp.int32, lse.shape, 0)
    own = jnp.sum(jnp.where(shard == place_ref[1], lse, 0.0), axis=0, keepdims=True)
    loss = jnp.sum(lse - pos, axis=0, keepdims=True)
    for i in range(out_ref.shape[0]):
        out_ref[i, 0:1, :] = own
        out_ref[i, 1:2, :] = loss


def grad_kernel(s_ref, b_ref, lse_ref, others_ref, mates_ref, out_ref, loss_ref, d_ref):
    step = pl.program_id(0)
    lanes = 128
    per = BLOCK // lanes
    for i in range(per):
        rows = slice(i * lanes, (i + 1) * lanes)
        mates = to_column(mates_ref[pl.ds(step * per + i, 1), :])
        own = to_column(lse_ref[pl.ds(step * per + i, 1), :])
        lane = lax.broadcasted_iota(jnp.int32, (lanes, lanes), 1)
        for t in range(others_ref.shape[0]):
            cols = slice(t * lanes, (t + 1) * lanes)
            s = s_ref[rows, cols]
            mate = jnp.where(lane == mates - t * lanes, 1.0, 0.0)
            d = (jnp.exp(s - own) - mate) + (jnp.exp(s - others_ref[t, 0:1, :]) - mate)
            d_ref[rows, cols] = d.astype(BF16)
    out_ref[...] = jnp.dot(d_ref[...], b_ref[...], preferred_element_type=F32).astype(BF16)
    total = jnp.sum(others_ref[:, 1, :], axis=0, keepdims=True)
    loss_ref[...] = jnp.sum(total, axis=1, keepdims=True)


def final_kernel(scale_ref, x_ref, parts_ref, out_ref):
    flat = x_ref[...].astype(F32)
    inv = lax.rsqrt(jnp.sum(flat * flat, axis=1, keepdims=True) + 1e-06)
    unit = flat * inv
    dunit = parts_ref[0].astype(F32)
    for i in range(1, parts_ref.shape[0]):
        dunit = dunit + parts_ref[i].astype(F32)
    dunit = dunit * scale_ref[0]
    out_ref[...] = inv * (dunit - unit * jnp.sum(unit * dunit, axis=1, keepdims=True))


def shape(dims, dtype):
    return jax.ShapeDtypeStruct(dims, dtype)


def body(embeddings, partner, inv_temp):
    views, width = embeddings.shape
    n_row, n_col = lax.axis_size("row"), lax.axis_size("col")
    n_a, n_b, total = n_col * views, n_row * views, n_row * n_col * views
    row_pos, col_pos = lax.axis_index("row"), lax.axis_index("col")
    place = jnp.stack([row_pos, col_pos]).astype(jnp.int32)

    unit_b, copies = pl.pallas_call(
        unit_kernel,
        out_shape=[shape((views, width), BF16), shape((n_col, views, width), BF16)],
        in_specs=[VMEM],
        out_specs=[VMEM, VMEM],
    )(embeddings)
    block_b = lax.all_gather(unit_b, "row", axis=0, tiled=True)
    block_a = lax.all_to_all(copies, "col", 0, 0, tiled=True).reshape(n_a, width)
    shard, lane = partner // views, partner % views
    local = shard // n_col * views + lane
    dest = jnp.arange(n_col, dtype=jnp.int32)[:, None]
    sent = jnp.where((shard % n_col)[None, :] == dest, local[None, :], -(1 << 20))
    mates = lax.all_to_all(sent.reshape(n_col, 1, views), "col", 0, 0, tiled=True).reshape(n_col, views)

    steps = (n_a // BLOCK,)
    params = pltpu.CompilerParams(vmem_limit_bytes=48 << 20)
    whole = lambda *dims: pl.BlockSpec(dims, lambda i: (0,) * len(dims))
    scores, stats = pl.pallas_call(
        score_kernel,
        grid=steps,
        out_shape=[shape((n_a, n_b), F32), shape((n_col, 3, n_col, views), F32)],
        in_specs=[SMEM, SMEM, pl.BlockSpec((BLOCK, width), lambda i: (i, 0)), whole(n_b, width), whole(n_col, views)],
        out_specs=[pl.BlockSpec((BLOCK, n_b), lambda i: (i, 0)), whole(n_col, 3, n_col, views)],
        compiler_params=params,
    )(place, inv_temp, block_a, block_b, mates)
    stats = lax.all_to_all(stats, "col", 0, 0, tiled=True)
    lse, own = pl.pallas_call(
        merge_kernel,
        out_shape=[shape((n_col, views), F32), shape((n_row, 2, views), F32)],
        in_specs=[SMEM, VMEM],
        out_specs=[VMEM, VMEM],
    )(place, stats)
    others = lax.all_to_all(own, "row", 0, 0, tiled=True)
    grads, loss = pl.pallas_call(
        grad_kernel,
        grid=steps,
        out_shape=[shape((n_a, width), BF16), shape((1, 1), F32)],
        in_specs=[
            pl.BlockSpec((BLOCK, n_b), lambda i: (i, 0)),
            whole(n_b, width),
            whole(n_col, views),
            whole(n_row, 2, views),
            whole(n_col, views),
        ],
        out_specs=[pl.BlockSpec((BLOCK, width), lambda i: (i, 0)), whole(1, 1)],
        scratch_shapes=[pltpu.VMEM((BLOCK, n_b), BF16)],
        compiler_params=params,
    )(scores, block_b, lse, others, mates)
    parts = lax.all_to_all(grads.reshape(n_col, views, width), "col", 0, 0, tiled=True)
    grad_embed = pl.pallas_call(
        final_kernel,
        out_shape=shape((views, width), F32),
        in_specs=[SMEM, VMEM, VMEM],
        out_specs=VMEM,
    )(inv_temp / total, embeddings, parts)
    return (loss / total).reshape(1), grad_embed


def solution(mesh):
    in_specs = (P(("row", "col"), None), P(("row", "col")), P())
    out_specs = (P(), P(("row", "col"), None))
    return jax.shard_map(body, mesh=mesh, in_specs=in_specs, out_specs=out_specs, check_vma=False)
```

```python
import functools

import jax
import jax.numpy as jnp
from jax import lax
from jax.experimental import pallas as pl
from jax.experimental.pallas import tpu as pltpu
from jax.sharding import PartitionSpec as P

F32 = jnp.float32
BF16 = jnp.bfloat16
I32 = jnp.int32
LANES = 128
EXTRA = 8
BLOCK = 256
VMEM_LIMIT = 36 << 20
AXES = ("row", "col")
VMEM = pl.BlockSpec(memory_space=pltpu.VMEM)
SMEM = pl.BlockSpec(memory_space=pltpu.SMEM)
ANY = pl.BlockSpec(memory_space=pl.ANY)


def device_id(x, y, z, core):
    return ((x % 4) * 4 + (y % 2) * 2 + core) * 8 + (y % 4) // 2 * 4 + z % 4


def mate_a(y):
    return y ^ 1


def mate_b(y):
    return (y + 1) % 4 if y % 2 else (y - 1) % 4


def to(where):
    pairs = []
    for x in range(4):
        for y in range(4):
            for z in range(4):
                for k in range(2):
                    pairs.append((device_id(x, y, z, k), device_id(*where(x, y, z, k, 1 - 2 * k))))
    return pairs


SWAP = to(lambda x, y, z, k, g: (x, y, z, 1 - k))
ALONG_Z = to(lambda x, y, z, k, g: (x, y, z + g, k))
ALONG_X = to(lambda x, y, z, k, g: (x + g, y, z, k))
ALONG_YZ = to(lambda x, y, z, k, g: (x, mate_a(y), z + g, k))
ALONG_XY = to(lambda x, y, z, k, g: (x + g, mate_b(y), z, k))
ALONG_Y = to(lambda x, y, z, k, g: (x, mate_b(y) if k else mate_a(y), z, k))

PARTNER_A = to(lambda x, y, z, k, g: (x, mate_a(y), z, k))
PARTNER_B = to(lambda x, y, z, k, g: (x, mate_b(y), z, k))
FROM_Z = [to(lambda x, y, z, k, g, d=d: (x, y, z - d, k)) for d in (1, 2, 3)]
FROM_X = [to(lambda x, y, z, k, g, d=d: (x - d, y, z, k)) for d in (1, 2, 3)]

GROUPS_A = [
    [device_id(x, y, z, k) for y in (p, p + 1) for z in range(4)] for x in range(4) for p in (0, 2) for k in range(2)
]
COLUMNS = [
    (0, 0, 0), (0, 0, 1), (-1, 0, 0), (-1, 0, 1), (-1, 1, 0), (-1, 1, 1), (1, 0, 1), (1, 0, 0),
    (1, 1, 1), (1, 1, 0), (2, 0, 0), (2, 1, 0), (2, 0, 1), (2, 1, 1), (0, 1, 0), (0, 1, 1),
]


def eye(n):
    return lax.broadcasted_iota(I32, (n, n), 0) == lax.broadcasted_iota(I32, (n, n), 1)


def to_column(row):
    return jnp.sum(jnp.where(eye(row.shape[1]), row, jnp.zeros_like(row)), axis=1, keepdims=True)


def to_row(column):
    return jnp.sum(jnp.where(eye(column.shape[0]), column, jnp.zeros_like(column)), axis=0, keepdims=True)


def unit_kernel(x_ref, mates_ref, out_ref):
    flat = x_ref[...].astype(F32)
    inv = lax.rsqrt(jnp.sum(flat * flat, axis=1, keepdims=True) + 1e-06)
    out_ref[0:LANES, :] = (flat * inv).astype(BF16)
    mates = mates_ref[...]
    row = jnp.concatenate([mates >> 7, mates & 127, jnp.zeros((1, out_ref.shape[1] - 2 * LANES), I32)], axis=1)
    out_ref[LANES:, :] = jnp.broadcast_to(row.astype(F32), (2 * EXTRA, row.shape[1])).astype(BF16)


def score_kernel(
    place, scale_ref, own, rz, d_a, fz, s_z, ry, s_ry, rx, d_b, s_rx, s_db, fx, s_fx,
    s_ref, b_ref, stats_ref, mates_ref, a_ref,
):
    core, y, z = place[0], place[1], place[2]
    scale = scale_ref[0]
    n, e = LANES, 2 * LANES

    def put(ref, at, src, start, rows=n):
        ref[at * n : at * n + rows, :] = src[start : start + rows, :]

    put(a_ref, 0, own, 0)
    put(a_ref, 1, rz, 0)
    put(a_ref, 2, d_a, 0)
    put(a_ref, 3, fz, 0, e)
    put(a_ref, 5, s_z, 0, e)
    for src, at in ((own, 0), (rx, 2), (d_b, 4), (s_rx, 6), (s_db, 8), (fx, 10), (s_fx, 12)):
        put(b_ref, at, src, 0, e)

    @pl.when(core == 0)
    def _():
        put(a_ref, 7, ry, 0)
        put(b_ref, 14, s_ry, n)
        put(b_ref, 15, s_ry, 0)

    @pl.when(core == 1)
    def _():
        put(a_ref, 7, s_ry, n)
        put(b_ref, 14, ry, 0, e)

    tail = lambda src: src[e : e + 2 * EXTRA, 0 : 2 * n].astype(F32)
    tails = [tail(src) for src in (own, rz, d_a, fz, s_z, ry, s_ry)]
    head = [(0, 0), (1, 0), (2, 0), (3, 0), (3, EXTRA), (4, 0), (4, EXTRA)]
    rows = [tails[p][r : r + 1] for p, r in head]
    rows.append(jnp.where(core == 0, tails[5][0:1], tails[6][EXTRA : EXTRA + 1]))
    rows = jnp.concatenate(rows, axis=0).astype(I32)
    shard, lane = rows[:, 0:n], rows[:, n:]
    mate_x, mate_k, mate_z = shard >> 5, (shard >> 3) & 1, shard & 3
    mate_y = ((shard >> 2) & 1) * 2 + ((shard >> 4) & 1)
    slot = (1 - (mate_y & 1)) * 4 + mate_x + jnp.where(mate_k == core, 0, 8)
    local = jnp.zeros_like(slot)
    for t in range(16):
        local = jnp.where(slot == place[11 + t], t * n + lane, local)
    here = (mate_z == z) & ((((mate_y + 1) & 3) >> 1) == (((y + 1) & 3) >> 1))
    mates_ref[...] = jnp.where(here, local, -1)

    n_a, n_b = s_ref.shape
    wide = 512
    per = BLOCK // n

    def scores_of(step):
        a = a_ref[step * BLOCK : (step + 1) * BLOCK, :]
        for j in range(n_b // wide):
            b = b_ref[j * wide : (j + 1) * wide, :]
            part = lax.dot_general(a, b, (((1,), (1,)), ((), ())), preferred_element_type=F32) * scale
            if step == 0 and j == 0:
                r = lax.broadcasted_iota(I32, (BLOCK, wide), 0)
                c = lax.broadcasted_iota(I32, (BLOCK, wide), 1)
                part = jnp.where((r == c) & (r < n), -jnp.inf, part)
            s_ref[step * BLOCK : (step + 1) * BLOCK, j * wide : (j + 1) * wide] = part

    def stats_of(step):
        lane = lax.broadcasted_iota(I32, (n, n), 1)
        for i in range(per):
            shard = step * per + i
            rows = slice(shard * n, (shard + 1) * n)
            mates = to_column(mates_ref[shard : shard + 1, :])
            peak = s_ref[rows, 0:n]
            for t in range(1, n_b // n):
                peak = jnp.maximum(peak, s_ref[rows, t * n : (t + 1) * n])
            peak = jnp.max(peak, axis=1, keepdims=True)
            sums = jnp.zeros((n, n), F32)
            pos = jnp.zeros((n, n), F32)
            for t in range(n_b // n):
                s = s_ref[rows, t * n : (t + 1) * n]
                sums = sums + jnp.exp(s - peak)
                pos = pos + jnp.where(lane == mates - t * n, s, 0.0)
            values = (peak, jnp.sum(sums, axis=1, keepdims=True), jnp.sum(pos, axis=1, keepdims=True))
            for q, value in enumerate(values):
                value = to_row(value)
                stats_ref[q, pl.ds(place[3 + shard], 1), :] = value

    steps = n_a // BLOCK
    scores_of(0)
    for step in range(steps):
        if step + 1 < steps:
            scores_of(step + 1)
        stats_of(step)


def merge_kernel(place, g0, g1, g2, g3, lse_ref, out_ref):
    y, z = place[1], place[2]
    parts = []
    for slot in range(8):
        turn = jnp.where((y & 1) == slot // 4, 0, 1)
        step = (slot % 4 - z) & 3
        part = g0[turn]
        for d, g in ((1, g1), (2, g2), (3, g3)):
            part = jnp.where(step == d, g[turn], part)
        parts.append(part)
    peak = parts[0][0]
    for part in parts[1:]:
        peak = jnp.maximum(peak, part[0])
    total = jnp.zeros_like(peak)
    pos = jnp.zeros_like(peak)
    for part in parts:
        total = total + part[1] * jnp.exp(part[0] - peak)
        pos = pos + part[2]
    lse = peak + jnp.log(total)
    lse_ref[...] = lse
    shard = lax.broadcasted_iota(I32, lse.shape, 0)
    out_ref[0:1, :] = jnp.sum(jnp.where(shard == place[3], lse, 0.0), axis=0, keepdims=True)
    out_ref[1:2, :] = jnp.sum(lse - pos, axis=0, keepdims=True)


def grad_kernel(
    place, s_ref, b_ref, lse_ref, h0, h1, h2, h3, mates_ref, out, loss_ref, d_ref, o_ref, sems
):
    n = LANES
    per = BLOCK // n
    n_a, n_b = s_ref.shape
    core, y, x = place[0], place[1], place[27]
    total = jnp.zeros((1, n), F32)
    for i in range(16):
        step = (i // 4 - x) & 3
        at = jnp.where((y >> 1) == i // 2 % 2, 0, 2) + jnp.where(core == i % 2, 0, 1)
        part = h0[at, 1:2, :]
        for d, h in ((1, h1), (2, h2), (3, h3)):
            part = jnp.where(step == d, h[at, 1:2, :], part)
        total = total + part
    loss_ref[...] = jnp.sum(total, axis=1, keepdims=True)
    copies = []
    lane = lax.broadcasted_iota(I32, (n, n), 1)

    forward = jnp.where(core == 0, 1, 0)

    def other_lse(t):
        turn, twin = COLUMNS[t][1:]
        at = 2 * turn + twin
        if COLUMNS[t][0] == 0:
            return h0[at, 0:1, :]
        if COLUMNS[t][0] == 2:
            return h2[at, 0:1, :]
        ahead, behind = h1[at, 0:1, :], h3[at, 0:1, :]
        return jnp.where(forward == (1 if COLUMNS[t][0] > 0 else 0), ahead, behind)

    others = [other_lse(t) for t in range(n_b // n)]

    def coefs_of(step):
        for i in range(per):
            shard = step * per + i
            rows = slice(shard * n, (shard + 1) * n)
            mates = to_column(mates_ref[shard : shard + 1, :])
            mine = to_column(lse_ref[pl.ds(place[3 + shard], 1), :])
            for t in range(n_b // n):
                cols = slice(t * n, (t + 1) * n)
                s = s_ref[rows, cols]
                mate = jnp.where(lane == mates - t * n, 1.0, 0.0)
                d = (jnp.exp(s - mine) - mate) + (jnp.exp(s - others[t]) - mate)
                d_ref[rows, cols] = d.astype(BF16)

    def grads_of(step):
        rows = slice(step * BLOCK, (step + 1) * BLOCK)
        o_ref[rows, :] = jnp.dot(d_ref[rows, :], b_ref[...], preferred_element_type=F32).astype(BF16)
        for i in range(per):
            shard = step * per + i
            copies.append(pltpu.make_async_copy(o_ref.at[pl.ds(shard * n, n)], out.at[place[3 + shard]], sems.at[shard]))
            copies[-1].start()

    steps = n_a // BLOCK
    coefs_of(0)
    for step in range(steps):
        if step + 1 < steps:
            coefs_of(step + 1)
        grads_of(step)
    for copy in copies:
        copy.wait()


def final_kernel(scale_ref, x_ref, parts_ref, out_ref):
    flat = x_ref[...].astype(F32)
    inv = lax.rsqrt(jnp.sum(flat * flat, axis=1, keepdims=True) + 1e-06)
    unit = flat * inv
    dunit = parts_ref[0].astype(F32)
    for i in range(1, parts_ref.shape[0]):
        dunit = dunit + parts_ref[i].astype(F32)
    dunit = dunit * scale_ref[0]
    out_ref[...] = inv * (dunit - unit * jnp.sum(unit * dunit, axis=1, keepdims=True))


def shape(dims, dtype):
    return jax.ShapeDtypeStruct(dims, dtype)


def body(embeddings, partner, inv_temp):
    views, width = embeddings.shape
    row, col = lax.axis_index("row").astype(I32), lax.axis_index("col").astype(I32)
    x, core, z = row >> 2, row & 1, col & 3
    y = (col >> 2) * 2 + ((row >> 1) & 1)
    sign = 1 - 2 * core
    other_y = jnp.where((y & 1) == 1, y + 1, y - 1) & 3
    slot_a = lambda yy, zz: (yy & 1) * 4 + (zz & 3)
    slot_b = lambda xx, yy, same: (1 - (yy & 1)) * 4 + (xx & 3) + (0 if same else 8)
    slots_a = [
        slot_a(y, z), slot_a(y, z - sign), slot_a(y ^ 1, z - sign), slot_a(y, z + 2),
        slot_a(y ^ 1, z + 2), slot_a(y, z + sign), slot_a(y ^ 1, z + sign), slot_a(y ^ 1, z),
    ]
    slots_b = [
        slot_b(x, y, True), slot_b(x, y, False),
        slot_b(x - sign, y, True), slot_b(x - sign, y, False),
        slot_b(x - sign, other_y, True), slot_b(x - sign, other_y, False),
        slot_b(x + sign, y, False), slot_b(x + sign, y, True),
        slot_b(x + sign, other_y, False), slot_b(x + sign, other_y, True),
        slot_b(x + 2, y, True), slot_b(x + 2, other_y, True),
        slot_b(x + 2, y, False), slot_b(x + 2, other_y, False),
        slot_b(x, other_y, True), slot_b(x, other_y, False),
    ]
    place = jnp.stack([core, y, z, *slots_a, *slots_b, x]).astype(I32)
    send = lambda v, pairs: lax.ppermute(v, AXES, pairs)
    n = LANES
    params = pltpu.CompilerParams(vmem_limit_bytes=VMEM_LIMIT)

    mine = pl.pallas_call(
        unit_kernel, out_shape=shape((views + 2 * EXTRA, width), BF16), in_specs=[VMEM, VMEM], out_specs=VMEM
    )(embeddings, partner.reshape(1, views))
    twin = send(mine, SWAP)
    own = jnp.concatenate([mine[:n], twin[:n], mine[n : n + EXTRA], twin[n : n + EXTRA]], axis=0)
    both = own[: 2 * n]
    d_a = send(own, ALONG_YZ)
    d_b = send(both, ALONG_XY)
    rz = send(own, ALONG_Z)
    rx = send(both, ALONG_X)
    ry = send(own, ALONG_Y)
    e = 2 * n
    fz = send(jnp.concatenate([rz[:n], d_a[:n], rz[e : e + EXTRA], d_a[e : e + EXTRA]], axis=0), ALONG_Z)
    fx = send(jnp.concatenate([rx[:n], d_b[:n]], axis=0), ALONG_X)
    s_rx, s_db, s_ry = send(rx, SWAP), send(d_b, SWAP), send(ry, SWAP)
    s_z = send(jnp.concatenate([rz[n:e], d_a[n:e], rz[e + EXTRA :], d_a[e + EXTRA :]], axis=0), SWAP)
    s_fx = send(fx, SWAP)

    n_a, n_b = 8 * views, 16 * views
    fast = lambda v: pltpu.with_memory_space_constraint(v, pltpu.VMEM)
    pieces = [fast(v) for v in (own, rz, d_a, fz, s_z, ry, s_ry, rx, d_b, s_rx, s_db, fx, s_fx)]
    scores, block_b, stats, mates = pl.pallas_call(
        score_kernel,
        out_shape=[
            pltpu.VMEM((n_a, n_b), F32),
            pltpu.VMEM((n_b, width), BF16),
            shape((3, 8, views), F32),
            shape((8, views), I32),
        ],
        in_specs=[SMEM, SMEM] + [VMEM] * 13,
        out_specs=[VMEM] * 4,
        scratch_shapes=[pltpu.VMEM((n_a, width), BF16)],
        compiler_params=params,
    )(place, inv_temp, *pieces)
    pair = jnp.stack([stats, send(stats, PARTNER_A)])
    g1, g2, g3 = (send(pair, pairs) for pairs in FROM_Z)
    lse, spread = pl.pallas_call(
        merge_kernel,
        out_shape=[shape((8, views), F32), shape((2, views), F32)],
        in_specs=[SMEM] + [VMEM] * 4,
        out_specs=[VMEM, VMEM],
    )(place, pair, g1, g2, g3)
    twins = jnp.stack([spread, send(spread, SWAP)])
    four = jnp.concatenate([twins, send(twins, PARTNER_B)], axis=0)
    h1, h2, h3 = (send(four, pairs) for pairs in FROM_X)
    grads, loss = pl.pallas_call(
        grad_kernel,
        out_shape=[shape((8, views, width), BF16), shape((1, 1), F32)],
        in_specs=[SMEM] + [VMEM] * 8,
        out_specs=[ANY, VMEM],
        scratch_shapes=[
            pltpu.VMEM((n_a, n_b), BF16),
            pltpu.VMEM((n_a, width), BF16),
            pltpu.SemaphoreType.DMA((8,)),
        ],
        compiler_params=params,
    )(place, fast(scores), fast(block_b), lse, four, h1, h2, h3, mates)
    parts = lax.all_to_all(grads, AXES, 0, 0, tiled=True, axis_index_groups=GROUPS_A)
    total = views * 128
    grad_embed = pl.pallas_call(
        final_kernel,
        out_shape=shape((views, width), F32),
        in_specs=[SMEM, VMEM, VMEM],
        out_specs=VMEM,
    )(inv_temp / total, embeddings, parts)
    return (loss / total).reshape(1), grad_embed


def solution(mesh):
    in_specs = (P(("row", "col"), None), P(("row", "col")), P())
    out_specs = (P(), P(("row", "col"), None))
    return jax.shard_map(body, mesh=mesh, in_specs=in_specs, out_specs=out_specs, check_vma=False)
```

```python
import functools

import jax
import jax.numpy as jnp
from jax import lax
from jax.experimental import pallas as pl
from jax.experimental.pallas import tpu as pltpu
from jax.sharding import PartitionSpec as P

F32 = jnp.float32
BF16 = jnp.bfloat16
I32 = jnp.int32
LANES = 128
EXTRA = 8
BLOCK = 256
VMEM_LIMIT = 36 << 20
AXES = ("row", "col")
VMEM = pl.BlockSpec(memory_space=pltpu.VMEM)
SMEM = pl.BlockSpec(memory_space=pltpu.SMEM)
ANY = pl.BlockSpec(memory_space=pl.ANY)


def device_id(x, y, z, core):
    return ((x % 4) * 4 + (y % 2) * 2 + core) * 8 + (y % 4) // 2 * 4 + z % 4


def mate_a(y):
    return y ^ 1


def mate_b(y):
    return (y + 1) % 4 if y % 2 else (y - 1) % 4


def to(where):
    pairs = []
    for x in range(4):
        for y in range(4):
            for z in range(4):
                for k in range(2):
                    pairs.append((device_id(x, y, z, k), device_id(*where(x, y, z, k, 1 - 2 * k))))
    return pairs


SWAP = to(lambda x, y, z, k, g: (x, y, z, 1 - k))
ALONG_Z = to(lambda x, y, z, k, g: (x, y, z + g, k))
ALONG_X = to(lambda x, y, z, k, g: (x + g, y, z, k))
ALONG_YZ = to(lambda x, y, z, k, g: (x, mate_a(y), z + g, k))
ALONG_XY = to(lambda x, y, z, k, g: (x + g, mate_b(y), z, k))
ALONG_Y = to(lambda x, y, z, k, g: (x, mate_b(y) if k else mate_a(y), z, k))

PARTNER_A = to(lambda x, y, z, k, g: (x, mate_a(y), z, k))
PARTNER_B = to(lambda x, y, z, k, g: (x, mate_b(y), z, k))
FROM_Z = [to(lambda x, y, z, k, g, d=d: (x, y, z - d, k)) for d in (1, 2, 3)]
FROM_X = [to(lambda x, y, z, k, g, d=d: (x - d, y, z, k)) for d in (1, 2, 3)]

OWNERS = [
    None,
    PARTNER_A,
    to(lambda x, y, z, k, g: (x, y, z - g, k)),
    ALONG_Z,
    to(lambda x, y, z, k, g: (x, y, z + 2, k)),
    ALONG_YZ,
    to(lambda x, y, z, k, g: (x, mate_a(y), z + 2, k)),
    to(lambda x, y, z, k, g: (x, mate_a(y), z - g, k)),
]

COLUMNS = [
    (0, 0, 0), (0, 0, 1), (-1, 0, 0), (-1, 0, 1), (-1, 1, 0), (-1, 1, 1), (1, 0, 1), (1, 0, 0),
    (1, 1, 1), (1, 1, 0), (2, 0, 0), (2, 1, 0), (2, 0, 1), (2, 1, 1), (0, 1, 0), (0, 1, 1),
]


def eye(n):
    return lax.broadcasted_iota(I32, (n, n), 0) == lax.broadcasted_iota(I32, (n, n), 1)


def to_column(row):
    return jnp.sum(jnp.where(eye(row.shape[1]), row, jnp.zeros_like(row)), axis=1, keepdims=True)


def to_row(column):
    return jnp.sum(jnp.where(eye(column.shape[0]), column, jnp.zeros_like(column)), axis=0, keepdims=True)


def unit_kernel(x_ref, mates_ref, out_ref):
    flat = x_ref[...].astype(F32)
    inv = lax.rsqrt(jnp.sum(flat * flat, axis=1, keepdims=True) + 1e-06)
    out_ref[0:LANES, :] = (flat * inv).astype(BF16)
    mates = mates_ref[...]
    row = jnp.concatenate([mates >> 7, mates & 127, jnp.zeros((1, out_ref.shape[1] - 2 * LANES), I32)], axis=1)
    out_ref[LANES:, :] = jnp.broadcast_to(row.astype(F32), (2 * EXTRA, row.shape[1])).astype(BF16)


def score_kernel(
    place, scale_ref, own, rz, d_a, fz, s_z, ry, s_ry, rx, d_b, s_rx, s_db, fx, s_fx,
    s_ref, b_ref, stats_ref, mates_ref, a_ref,
):
    core, y, z = place[0], place[1], place[2]
    scale = scale_ref[0]
    n, e = LANES, 2 * LANES

    def put(ref, at, src, start, rows=n):
        ref[at * n : at * n + rows, :] = src[start : start + rows, :]

    put(a_ref, 0, own, 0)
    put(a_ref, 2, rz, 0)
    put(a_ref, 3, s_z, 0)
    put(a_ref, 4, fz, 0)
    put(a_ref, 5, s_z, n)
    put(a_ref, 6, fz, n)
    put(a_ref, 7, d_a, 0)
    for src, at in ((own, 0), (rx, 2), (d_b, 4), (s_rx, 6), (s_db, 8), (fx, 10), (s_fx, 12)):
        put(b_ref, at, src, 0, e)

    @pl.when(core == 0)
    def _():
        put(a_ref, 1, ry, 0)
        put(b_ref, 14, s_ry, n)
        put(b_ref, 15, s_ry, 0)

    @pl.when(core == 1)
    def _():
        put(a_ref, 1, s_ry, n)
        put(b_ref, 14, ry, 0, e)

    tail = lambda src: src[e : e + 2 * EXTRA, 0 : 2 * n].astype(F32)
    tails = [tail(src) for src in (own, rz, d_a, fz, s_z, ry, s_ry)]
    head = [(0, 0), (1, 0), (4, 0), (3, 0), (4, EXTRA), (3, EXTRA), (2, 0)]
    rows = [tails[p][r : r + 1] for p, r in head]
    rows.insert(1, jnp.where(core == 0, tails[5][0:1], tails[6][EXTRA : EXTRA + 1]))
    rows = jnp.concatenate(rows, axis=0).astype(I32)
    shard, lane = rows[:, 0:n], rows[:, n:]
    mate_x, mate_k, mate_z = shard >> 5, (shard >> 3) & 1, shard & 3
    mate_y = ((shard >> 2) & 1) * 2 + ((shard >> 4) & 1)
    slot = (1 - (mate_y & 1)) * 4 + mate_x + jnp.where(mate_k == core, 0, 8)
    local = jnp.zeros_like(slot)
    for t in range(16):
        local = jnp.where(slot == place[11 + t], t * n + lane, local)
    here = (mate_z == z) & ((((mate_y + 1) & 3) >> 1) == (((y + 1) & 3) >> 1))
    mates_ref[...] = jnp.where(here, local, -1)

    n_a, n_b = s_ref.shape
    wide = 512
    per = BLOCK // n

    def scores_of(step):
        a = a_ref[step * BLOCK : (step + 1) * BLOCK, :]
        for j in range(n_b // wide):
            b = b_ref[j * wide : (j + 1) * wide, :]
            part = lax.dot_general(a, b, (((1,), (1,)), ((), ())), preferred_element_type=F32) * scale
            if step == 0 and j == 0:
                r = lax.broadcasted_iota(I32, (BLOCK, wide), 0)
                c = lax.broadcasted_iota(I32, (BLOCK, wide), 1)
                part = jnp.where((r == c) & (r < n), -jnp.inf, part)
            s_ref[step * BLOCK : (step + 1) * BLOCK, j * wide : (j + 1) * wide] = part

    def stats_of(step):
        lane = lax.broadcasted_iota(I32, (n, n), 1)
        for i in range(per):
            shard = step * per + i
            rows = slice(shard * n, (shard + 1) * n)
            mates = to_column(mates_ref[shard : shard + 1, :])
            peak = s_ref[rows, 0:n]
            for t in range(1, n_b // n):
                peak = jnp.maximum(peak, s_ref[rows, t * n : (t + 1) * n])
            peak = jnp.max(peak, axis=1, keepdims=True)
            sums = jnp.zeros((n, n), F32)
            pos = jnp.zeros((n, n), F32)
            for t in range(n_b // n):
                s = s_ref[rows, t * n : (t + 1) * n]
                sums = sums + jnp.exp(s - peak)
                pos = pos + jnp.where(lane == mates - t * n, s, 0.0)
            values = (peak, jnp.sum(sums, axis=1, keepdims=True), jnp.sum(pos, axis=1, keepdims=True))
            for q, value in enumerate(values):
                value = to_row(value)
                stats_ref[q, pl.ds(place[3 + shard], 1), :] = value

    steps = n_a // BLOCK
    scores_of(0)
    for step in range(steps):
        if step + 1 < steps:
            scores_of(step + 1)
        stats_of(step)


def merge_kernel(place, g0, g1, g2, g3, lse_ref, out_ref):
    y, z = place[1], place[2]
    parts = []
    for slot in range(8):
        turn = jnp.where((y & 1) == slot // 4, 0, 1)
        step = (slot % 4 - z) & 3
        part = g0[turn]
        for d, g in ((1, g1), (2, g2), (3, g3)):
            part = jnp.where(step == d, g[turn], part)
        parts.append(part)
    peak = parts[0][0]
    for part in parts[1:]:
        peak = jnp.maximum(peak, part[0])
    total = jnp.zeros_like(peak)
    pos = jnp.zeros_like(peak)
    for part in parts:
        total = total + part[1] * jnp.exp(part[0] - peak)
        pos = pos + part[2]
    lse = peak + jnp.log(total)
    lse_ref[...] = lse
    shard = lax.broadcasted_iota(I32, lse.shape, 0)
    out_ref[0:1, :] = jnp.sum(jnp.where(shard == place[3], lse, 0.0), axis=0, keepdims=True)
    out_ref[1:2, :] = jnp.sum(lse - pos, axis=0, keepdims=True)


def grad_kernel(which, place, s_ref, b_ref, lse_ref, h0, h1, h2, h3, mates_ref, *refs):
    n = LANES
    per = BLOCK // n
    n_b = s_ref.shape[1]
    outs, d_ref = refs[:per], refs[-1]
    if which == 0:
        core, y, x = place[0], place[1], place[27]
        total = jnp.zeros((1, n), F32)
        for i in range(16):
            step = (i // 4 - x) & 3
            at = jnp.where((y >> 1) == i // 2 % 2, 0, 2) + jnp.where(core == i % 2, 0, 1)
            part = h0[at, 1:2, :]
            for d, h in ((1, h1), (2, h2), (3, h3)):
                part = jnp.where(step == d, h[at, 1:2, :], part)
            total = total + part
        refs[per][...] = jnp.sum(total, axis=1, keepdims=True)
    core = place[0]
    lane = lax.broadcasted_iota(I32, (n, n), 1)

    forward = jnp.where(core == 0, 1, 0)

    def other_lse(t):
        turn, twin = COLUMNS[t][1:]
        at = 2 * turn + twin
        if COLUMNS[t][0] == 0:
            return h0[at, 0:1, :]
        if COLUMNS[t][0] == 2:
            return h2[at, 0:1, :]
        ahead, behind = h1[at, 0:1, :], h3[at, 0:1, :]
        return jnp.where(forward == (1 if COLUMNS[t][0] > 0 else 0), ahead, behind)

    others = [other_lse(t) for t in range(n_b // n)]

    for i in range(per):
        shard = which * per + i
        mates = to_column(mates_ref[shard : shard + 1, :])
        mine = to_column(lse_ref[pl.ds(place[3 + shard], 1), :])
        for t in range(n_b // n):
            cols = slice(t * n, (t + 1) * n)
            s = s_ref[shard * n : (shard + 1) * n, cols]
            mate = jnp.where(lane == mates - t * n, 1.0, 0.0)
            d = (jnp.exp(s - mine) - mate) + (jnp.exp(s - others[t]) - mate)
            d_ref[i * n : (i + 1) * n, cols] = d.astype(BF16)
    out = jnp.dot(d_ref[...], b_ref[...], preferred_element_type=F32).astype(BF16)
    for i in range(per):
        outs[i][...] = out[i * n : (i + 1) * n]


def final_kernel(scale_ref, x_ref, *refs):
    parts, out_ref = refs[:-1], refs[-1]
    flat = x_ref[...].astype(F32)
    inv = lax.rsqrt(jnp.sum(flat * flat, axis=1, keepdims=True) + 1e-06)
    unit = flat * inv
    dunit = parts[0][...].astype(F32)
    for part in parts[1:]:
        dunit = dunit + part[...].astype(F32)
    dunit = dunit * scale_ref[0]
    out_ref[...] = inv * (dunit - unit * jnp.sum(unit * dunit, axis=1, keepdims=True))


def shape(dims, dtype):
    return jax.ShapeDtypeStruct(dims, dtype)


def body(embeddings, partner, inv_temp):
    views, width = embeddings.shape
    row, col = lax.axis_index("row").astype(I32), lax.axis_index("col").astype(I32)
    x, core, z = row >> 2, row & 1, col & 3
    y = (col >> 2) * 2 + ((row >> 1) & 1)
    sign = 1 - 2 * core
    other_y = jnp.where((y & 1) == 1, y + 1, y - 1) & 3
    slot_a = lambda yy, zz: (yy & 1) * 4 + (zz & 3)
    slot_b = lambda xx, yy, same: (1 - (yy & 1)) * 4 + (xx & 3) + (0 if same else 8)
    slots_a = [
        slot_a(y, z), slot_a(y ^ 1, z), slot_a(y, z - sign), slot_a(y, z + sign),
        slot_a(y, z + 2), slot_a(y ^ 1, z + sign), slot_a(y ^ 1, z + 2), slot_a(y ^ 1, z - sign),
    ]
    slots_b = [
        slot_b(x, y, True), slot_b(x, y, False),
        slot_b(x - sign, y, True), slot_b(x - sign, y, False),
        slot_b(x - sign, other_y, True), slot_b(x - sign, other_y, False),
        slot_b(x + sign, y, False), slot_b(x + sign, y, True),
        slot_b(x + sign, other_y, False), slot_b(x + sign, other_y, True),
        slot_b(x + 2, y, True), slot_b(x + 2, other_y, True),
        slot_b(x + 2, y, False), slot_b(x + 2, other_y, False),
        slot_b(x, other_y, True), slot_b(x, other_y, False),
    ]
    place = jnp.stack([core, y, z, *slots_a, *slots_b, x]).astype(I32)
    send = lambda v, pairs: lax.ppermute(v, AXES, pairs)
    n = LANES
    params = pltpu.CompilerParams(vmem_limit_bytes=VMEM_LIMIT)
    small = pltpu.CompilerParams(vmem_limit_bytes=8 << 20)

    mine = pl.pallas_call(
        unit_kernel, out_shape=shape((views + 2 * EXTRA, width), BF16), in_specs=[VMEM, VMEM], out_specs=VMEM, compiler_params=small
    )(embeddings, partner.reshape(1, views))
    twin = send(mine, SWAP)
    own = jnp.concatenate([mine[:n], twin[:n], mine[n : n + EXTRA], twin[n : n + EXTRA]], axis=0)
    d_a = send(own, ALONG_YZ)
    d_b = send(own, ALONG_XY)
    rz = send(own, ALONG_Z)
    rx = send(own, ALONG_X)
    ry = send(own, ALONG_Y)
    e = 2 * n
    fz = send(jnp.concatenate([rz[:n], d_a[:n], rz[e : e + EXTRA], d_a[e : e + EXTRA]], axis=0), ALONG_Z)
    fx = send(jnp.concatenate([rx[:n], d_b[:n]], axis=0), ALONG_X)
    s_rx, s_db, s_ry = send(rx, SWAP), send(d_b, SWAP), send(ry, SWAP)
    s_z = send(jnp.concatenate([rz[n:e], d_a[n:e], rz[e + EXTRA :], d_a[e + EXTRA :]], axis=0), SWAP)
    s_fx = send(fx, SWAP)

    n_a, n_b = 8 * views, 16 * views
    fast = lambda v: pltpu.with_memory_space_constraint(v, pltpu.VMEM)
    pieces = [fast(v) for v in (own, rz, d_a, fz, s_z, ry, s_ry, rx, d_b, s_rx, s_db, fx, s_fx)]
    scores, block_b, stats, mates = pl.pallas_call(
        score_kernel,
        out_shape=[
            pltpu.VMEM((n_a, n_b), F32),
            pltpu.VMEM((n_b, width), BF16),
            shape((3, 8, views), F32),
            shape((8, views), I32),
        ],
        in_specs=[SMEM, SMEM] + [VMEM] * 13,
        out_specs=[VMEM] * 4,
        scratch_shapes=[pltpu.VMEM((n_a, width), BF16)],
        compiler_params=params,
    )(place, inv_temp, *pieces)
    pair = jnp.stack([stats, send(stats, PARTNER_A)])
    g1, g2, g3 = (send(pair, pairs) for pairs in FROM_Z)
    lse, spread = pl.pallas_call(
        merge_kernel,
        out_shape=[shape((8, views), F32), shape((2, views), F32)],
        in_specs=[SMEM] + [VMEM] * 4,
        out_specs=[VMEM, VMEM],
        compiler_params=small,
    )(place, pair, g1, g2, g3)
    twins = jnp.stack([spread, send(spread, SWAP)])
    four = jnp.concatenate([twins, send(twins, PARTNER_B)], axis=0)
    h1, h2, h3 = (send(four, pairs) for pairs in FROM_X)
    scores, block_b = fast(scores), fast(block_b)
    parts = [None] * 8
    for step in reversed(range(4)):
        outs = [shape((views, width), BF16)] * 2 + ([shape((1, 1), F32)] if step == 0 else [])
        got = pl.pallas_call(
            functools.partial(grad_kernel, step),
            out_shape=outs,
            in_specs=[SMEM] + [VMEM] * 8,
            out_specs=[VMEM] * len(outs),
            scratch_shapes=[pltpu.VMEM((BLOCK, n_b), BF16)],
            compiler_params=pltpu.CompilerParams(vmem_limit_bytes=16 << 20),
            cost_estimate=pl.CostEstimate(flops=4 * BLOCK * n_b * width, bytes_accessed=1 << 20, transcendentals=0),
        )(place, scores, block_b, lse, four, h1, h2, h3, mates)
        for i in (1, 0):
            shard = 2 * step + i
            parts[shard] = send(got[i], OWNERS[shard]) if shard else got[i]
    loss = got[2]
    total = views * 128
    rows = views // 4
    block = pl.BlockSpec((rows, width), lambda i: (i, 0))
    grad_embed = pl.pallas_call(
        final_kernel,
        grid=(views // rows,),
        out_shape=shape((views, width), F32),
        in_specs=[SMEM] + [block] * 9,
        out_specs=block,
        compiler_params=small,
    )(inv_temp / total, embeddings, *parts)
    return (loss / total).reshape(1), grad_embed


def solution(mesh):
    in_specs = (P(("row", "col"), None), P(("row", "col")), P())
    out_specs = (P(), P(("row", "col"), None))
    return jax.shard_map(body, mesh=mesh, in_specs=in_specs, out_specs=out_specs, check_vma=False)
```

```python
import functools

import jax
import jax.numpy as jnp
from jax import lax
from jax.experimental import pallas as pl
from jax.experimental.pallas import tpu as pltpu
from jax.sharding import PartitionSpec as P

F32 = jnp.float32
BF16 = jnp.bfloat16
I32 = jnp.int32
LANES = 128
EXTRA = 8
BLOCK = 256
VMEM_LIMIT = 16 << 20
AXES = ("row", "col")
VMEM = pl.BlockSpec(memory_space=pltpu.VMEM)
SMEM = pl.BlockSpec(memory_space=pltpu.SMEM)
ANY = pl.BlockSpec(memory_space=pl.ANY)


def device_id(x, y, z, core):
    return ((x % 4) * 4 + (y % 2) * 2 + core) * 8 + (y % 4) // 2 * 4 + z % 4


def mate_a(y):
    return y ^ 1


def mate_b(y):
    return (y + 1) % 4 if y % 2 else (y - 1) % 4


def to(where):
    pairs = []
    for x in range(4):
        for y in range(4):
            for z in range(4):
                for k in range(2):
                    pairs.append((device_id(x, y, z, k), device_id(*where(x, y, z, k, 1 - 2 * k))))
    return pairs


SWAP = to(lambda x, y, z, k, g: (x, y, z, 1 - k))
ALONG_Z = to(lambda x, y, z, k, g: (x, y, z + g, k))
ALONG_X = to(lambda x, y, z, k, g: (x + g, y, z, k))
ALONG_YZ = to(lambda x, y, z, k, g: (x, mate_a(y), z + g, k))
ALONG_XY = to(lambda x, y, z, k, g: (x + g, mate_b(y), z, k))
ALONG_Y = to(lambda x, y, z, k, g: (x, mate_b(y) if k else mate_a(y), z, k))

PARTNER_A = to(lambda x, y, z, k, g: (x, mate_a(y), z, k))
PARTNER_B = to(lambda x, y, z, k, g: (x, mate_b(y), z, k))
FROM_Z = [to(lambda x, y, z, k, g, d=d: (x, y, z - d, k)) for d in (1, 2, 3)]
FROM_X = [to(lambda x, y, z, k, g, d=d: (x - d, y, z, k)) for d in (1, 2, 3)]

BACK_Z = to(lambda x, y, z, k, g: (x, y, z - g, k))
BACK_YZ = to(lambda x, y, z, k, g: (x, mate_a(y), z - g, k))

COLUMNS = [
    (0, 0, 0), (0, 0, 1), (-1, 0, 0), (-1, 0, 1), (-1, 1, 0), (-1, 1, 1), (1, 0, 1), (1, 0, 0),
    (1, 1, 1), (1, 1, 0), (2, 0, 0), (2, 1, 0), (2, 0, 1), (2, 1, 1), (0, 1, 0), (0, 1, 1),
]


def eye(n):
    return lax.broadcasted_iota(I32, (n, n), 0) == lax.broadcasted_iota(I32, (n, n), 1)


def to_column(row):
    return jnp.sum(jnp.where(eye(row.shape[1]), row, jnp.zeros_like(row)), axis=1, keepdims=True)


def to_row(column):
    return jnp.sum(jnp.where(eye(column.shape[0]), column, jnp.zeros_like(column)), axis=0, keepdims=True)


def unit_kernel(x_ref, mates_ref, out_ref):
    flat = x_ref[...].astype(F32)
    inv = lax.rsqrt(jnp.sum(flat * flat, axis=1, keepdims=True) + 1e-06)
    out_ref[0:LANES, :] = (flat * inv).astype(BF16)
    mates = mates_ref[...]
    row = jnp.concatenate([mates >> 7, mates & 127, jnp.zeros((1, out_ref.shape[1] - 2 * LANES), I32)], axis=1)
    out_ref[LANES:, :] = jnp.broadcast_to(row.astype(F32), (2 * EXTRA, row.shape[1])).astype(BF16)


def score_kernel(
    place, scale_ref, own, rz, d_a, fz, s_z, ry, s_ry, rx, d_b, s_rx, s_db, fx, s_fx,
    s_ref, b_ref, stats_ref, mates_ref, a_ref,
):
    core, y, z = place[0], place[1], place[2]
    scale = scale_ref[0]
    n, e = LANES, 2 * LANES

    def put(ref, at, src, start, rows=n):
        ref[at * n : at * n + rows, :] = src[start : start + rows, :]

    put(a_ref, 0, own, 0)
    put(a_ref, 2, rz, 0)
    put(a_ref, 3, s_z, n)
    put(a_ref, 4, s_z, 0)
    put(a_ref, 5, d_a, 0)
    put(a_ref, 6, fz, 0, e)
    for src, at in ((own, 0), (rx, 2), (d_b, 4), (s_rx, 6), (s_db, 8), (fx, 10), (s_fx, 12)):
        put(b_ref, at, src, 0, e)

    @pl.when(core == 0)
    def _():
        put(a_ref, 1, ry, 0)
        put(b_ref, 14, s_ry, n)
        put(b_ref, 15, s_ry, 0)

    @pl.when(core == 1)
    def _():
        put(a_ref, 1, s_ry, n)
        put(b_ref, 14, ry, 0, e)

    tail = lambda src: src[e : e + 2 * EXTRA, 0 : 2 * n].astype(F32)
    tails = [tail(src) for src in (own, rz, d_a, fz, s_z, ry, s_ry)]
    head = [(0, 0), (1, 0), (4, EXTRA), (4, 0), (2, 0), (3, 0), (3, EXTRA)]
    rows = [tails[p][r : r + 1] for p, r in head]
    rows.insert(1, jnp.where(core == 0, tails[5][0:1], tails[6][EXTRA : EXTRA + 1]))
    rows = jnp.concatenate(rows, axis=0).astype(I32)
    shard, lane = rows[:, 0:n], rows[:, n:]
    mate_x, mate_k, mate_z = shard >> 5, (shard >> 3) & 1, shard & 3
    mate_y = ((shard >> 2) & 1) * 2 + ((shard >> 4) & 1)
    slot = (1 - (mate_y & 1)) * 4 + mate_x + jnp.where(mate_k == core, 0, 8)
    local = jnp.zeros_like(slot)
    for t in range(16):
        local = jnp.where(slot == place[11 + t], t * n + lane, local)
    here = (mate_z == z) & ((((mate_y + 1) & 3) >> 1) == (((y + 1) & 3) >> 1))
    mates_ref[...] = jnp.where(here, local, -1)

    n_a, n_b = s_ref.shape
    wide = 512
    per = BLOCK // n

    def scores_of(step):
        a = a_ref[step * BLOCK : (step + 1) * BLOCK, :]
        for j in range(n_b // wide):
            b = b_ref[j * wide : (j + 1) * wide, :]
            part = lax.dot_general(a, b, (((1,), (1,)), ((), ())), preferred_element_type=F32) * scale
            if step == 0 and j == 0:
                r = lax.broadcasted_iota(I32, (BLOCK, wide), 0)
                c = lax.broadcasted_iota(I32, (BLOCK, wide), 1)
                part = jnp.where((r == c) & (r < n), -jnp.inf, part)
            s_ref[step * BLOCK : (step + 1) * BLOCK, j * wide : (j + 1) * wide] = part

    def stats_of(step):
        lane = lax.broadcasted_iota(I32, (n, n), 1)
        for i in range(per):
            shard = step * per + i
            rows = slice(shard * n, (shard + 1) * n)
            mates = to_column(mates_ref[shard : shard + 1, :])
            peak = s_ref[rows, 0:n]
            for t in range(1, n_b // n):
                peak = jnp.maximum(peak, s_ref[rows, t * n : (t + 1) * n])
            peak = jnp.max(peak, axis=1, keepdims=True)
            sums = jnp.zeros((n, n), F32)
            pos = jnp.zeros((n, n), F32)
            for t in range(n_b // n):
                s = s_ref[rows, t * n : (t + 1) * n]
                sums = sums + jnp.exp(s - peak)
                pos = pos + jnp.where(lane == mates - t * n, s, 0.0)
            values = (peak, jnp.sum(sums, axis=1, keepdims=True), jnp.sum(pos, axis=1, keepdims=True))
            for q, value in enumerate(values):
                value = to_row(value)
                stats_ref[q, pl.ds(place[3 + shard], 1), :] = value

    steps = n_a // BLOCK
    scores_of(0)
    for step in range(steps):
        if step + 1 < steps:
            scores_of(step + 1)
        stats_of(step)


def merge_kernel(place, g0, g1, g2, g3, lse_ref, out_ref):
    y, z = place[1], place[2]
    parts = []
    for slot in range(8):
        turn = jnp.where((y & 1) == slot // 4, 0, 1)
        step = (slot % 4 - z) & 3
        part = g0[turn]
        for d, g in ((1, g1), (2, g2), (3, g3)):
            part = jnp.where(step == d, g[turn], part)
        parts.append(part)
    peak = parts[0][0]
    for part in parts[1:]:
        peak = jnp.maximum(peak, part[0])
    total = jnp.zeros_like(peak)
    pos = jnp.zeros_like(peak)
    for part in parts:
        total = total + part[1] * jnp.exp(part[0] - peak)
        pos = pos + part[2]
    lse = peak + jnp.log(total)
    lse_ref[...] = lse
    shard = lax.broadcasted_iota(I32, lse.shape, 0)
    out_ref[0:1, :] = jnp.sum(jnp.where(shard == place[3], lse, 0.0), axis=0, keepdims=True)
    out_ref[1:2, :] = jnp.sum(lse - pos, axis=0, keepdims=True)


def grad_kernel(which, place, s_ref, b_ref, lse_ref, h0, h1, h2, h3, mates_ref, *refs):
    n = LANES
    per = BLOCK // n
    n_b = s_ref.shape[1]
    outs, d_ref = refs[per:] if which == 2 else refs, refs[-1]
    if which == 0:
        core, y, x = place[0], place[1], place[27]
        total = jnp.zeros((1, n), F32)
        for i in range(16):
            step = (i // 4 - x) & 3
            at = jnp.where((y >> 1) == i // 2 % 2, 0, 2) + jnp.where(core == i % 2, 0, 1)
            part = h0[at, 1:2, :]
            for d, h in ((1, h1), (2, h2), (3, h3)):
                part = jnp.where(step == d, h[at, 1:2, :], part)
            total = total + part
        refs[per][...] = jnp.sum(total, axis=1, keepdims=True)
    core = place[0]
    lane = lax.broadcasted_iota(I32, (n, n), 1)

    forward = jnp.where(core == 0, 1, 0)

    def other_lse(t):
        turn, twin = COLUMNS[t][1:]
        at = 2 * turn + twin
        if COLUMNS[t][0] == 0:
            return h0[at, 0:1, :]
        if COLUMNS[t][0] == 2:
            return h2[at, 0:1, :]
        ahead, behind = h1[at, 0:1, :], h3[at, 0:1, :]
        return jnp.where(forward == (1 if COLUMNS[t][0] > 0 else 0), ahead, behind)

    others = [other_lse(t) for t in range(n_b // n)]

    for i in range(per):
        shard = which * per + i
        mates = to_column(mates_ref[shard : shard + 1, :])
        mine = to_column(lse_ref[pl.ds(place[3 + shard], 1), :])
        for t in range(n_b // n):
            cols = slice(t * n, (t + 1) * n)
            s = s_ref[shard * n : (shard + 1) * n, cols]
            mate = jnp.where(lane == mates - t * n, 1.0, 0.0)
            d = (jnp.exp(s - mine) - mate) + (jnp.exp(s - others[t]) - mate)
            d_ref[i * n : (i + 1) * n, cols] = d.astype(BF16)
    out = jnp.dot(d_ref[...], b_ref[...], preferred_element_type=F32)
    for i in range(per):
        shard = out[i * n : (i + 1) * n]
        if which == 2:
            shard = shard + refs[i][...].astype(F32)
        outs[i][...] = shard.astype(BF16)


def final_kernel(scale_ref, x_ref, *refs):
    parts, out_ref = refs[:-1], refs[-1]
    flat = x_ref[...].astype(F32)
    inv = lax.rsqrt(jnp.sum(flat * flat, axis=1, keepdims=True) + 1e-06)
    unit = flat * inv
    dunit = parts[0][...].astype(F32)
    for part in parts[1:]:
        dunit = dunit + part[...].astype(F32)
    dunit = dunit * scale_ref[0]
    out_ref[...] = inv * (dunit - unit * jnp.sum(unit * dunit, axis=1, keepdims=True))


def shape(dims, dtype):
    return jax.ShapeDtypeStruct(dims, dtype)


def body(embeddings, partner, inv_temp):
    views, width = embeddings.shape
    row, col = lax.axis_index("row").astype(I32), lax.axis_index("col").astype(I32)
    x, core, z = row >> 2, row & 1, col & 3
    y = (col >> 2) * 2 + ((row >> 1) & 1)
    sign = 1 - 2 * core
    other_y = jnp.where((y & 1) == 1, y + 1, y - 1) & 3
    slot_a = lambda yy, zz: (yy & 1) * 4 + (zz & 3)
    slot_b = lambda xx, yy, same: (1 - (yy & 1)) * 4 + (xx & 3) + (0 if same else 8)
    slots_a = [
        slot_a(y, z), slot_a(y ^ 1, z), slot_a(y, z - sign), slot_a(y ^ 1, z + sign),
        slot_a(y, z + sign), slot_a(y ^ 1, z - sign), slot_a(y, z + 2), slot_a(y ^ 1, z + 2),
    ]
    slots_b = [
        slot_b(x, y, True), slot_b(x, y, False),
        slot_b(x - sign, y, True), slot_b(x - sign, y, False),
        slot_b(x - sign, other_y, True), slot_b(x - sign, other_y, False),
        slot_b(x + sign, y, False), slot_b(x + sign, y, True),
        slot_b(x + sign, other_y, False), slot_b(x + sign, other_y, True),
        slot_b(x + 2, y, True), slot_b(x + 2, other_y, True),
        slot_b(x + 2, y, False), slot_b(x + 2, other_y, False),
        slot_b(x, other_y, True), slot_b(x, other_y, False),
    ]
    place = jnp.stack([core, y, z, *slots_a, *slots_b, x]).astype(I32)
    send = lambda v, pairs: lax.ppermute(v, AXES, pairs)
    n = LANES
    params = pltpu.CompilerParams(vmem_limit_bytes=VMEM_LIMIT)
    small = pltpu.CompilerParams(vmem_limit_bytes=8 << 20)

    mine = pl.pallas_call(
        unit_kernel, out_shape=shape((views + 2 * EXTRA, width), BF16), in_specs=[VMEM, VMEM], out_specs=VMEM, compiler_params=small
    )(embeddings, partner.reshape(1, views))
    twin = send(mine, SWAP)
    own = jnp.concatenate([mine[:n], twin[:n], mine[n : n + EXTRA], twin[n : n + EXTRA]], axis=0)
    d_a = send(own, ALONG_YZ)
    d_b = send(own, ALONG_XY)
    rz = send(own, ALONG_Z)
    rx = send(own, ALONG_X)
    ry = send(own, ALONG_Y)
    e = 2 * n
    fz = send(jnp.concatenate([rz[:n], d_a[:n], rz[e : e + EXTRA], d_a[e : e + EXTRA]], axis=0), ALONG_Z)
    fx = send(jnp.concatenate([rx[:n], d_b[:n]], axis=0), ALONG_X)
    s_rx, s_db, s_ry = send(rx, SWAP), send(d_b, SWAP), send(ry, SWAP)
    s_z = send(jnp.concatenate([rz[n:e], d_a[n:e], rz[e + EXTRA :], d_a[e + EXTRA :]], axis=0), SWAP)
    s_fx = send(fx, SWAP)

    n_a, n_b = 8 * views, 16 * views
    fast = lambda v: pltpu.with_memory_space_constraint(v, pltpu.VMEM)
    pieces = [fast(v) for v in (own, rz, d_a, fz, s_z, ry, s_ry, rx, d_b, s_rx, s_db, fx, s_fx)]
    scores, block_b, stats, mates = pl.pallas_call(
        score_kernel,
        out_shape=[
            pltpu.VMEM((n_a, n_b), F32),
            pltpu.VMEM((n_b, width), BF16),
            shape((3, 8, views), F32),
            shape((8, views), I32),
        ],
        in_specs=[SMEM, SMEM] + [VMEM] * 13,
        out_specs=[VMEM] * 4,
        scratch_shapes=[pltpu.VMEM((n_a, width), BF16)],
        compiler_params=params,
    )(place, inv_temp, *pieces)
    pair = jnp.stack([stats, send(stats, PARTNER_A)])
    g1, g2, g3 = (send(pair, pairs) for pairs in FROM_Z)
    lse, spread = pl.pallas_call(
        merge_kernel,
        out_shape=[shape((8, views), F32), shape((2, views), F32)],
        in_specs=[SMEM] + [VMEM] * 4,
        out_specs=[VMEM, VMEM],
        compiler_params=small,
    )(place, pair, g1, g2, g3)
    twins = jnp.stack([spread, send(spread, SWAP)])
    four = jnp.concatenate([twins, send(twins, PARTNER_B)], axis=0)
    h1, h2, h3 = (send(four, pairs) for pairs in FROM_X)
    scores, block_b = fast(scores), fast(block_b)

    def part(which, outs, *more):
        return pl.pallas_call(
            functools.partial(grad_kernel, which),
            out_shape=outs,
            in_specs=[SMEM] + [VMEM] * (8 + len(more)),
            out_specs=[VMEM] * len(outs),
            scratch_shapes=[pltpu.VMEM((BLOCK, n_b), BF16)],
            compiler_params=pltpu.CompilerParams(vmem_limit_bytes=16 << 20),
            cost_estimate=pl.CostEstimate(flops=4 * BLOCK * n_b * width, bytes_accessed=1 << 20, transcendentals=0),
        )(place, scores, block_b, lse, four, h1, h2, h3, mates, *more)

    one = shape((views, width), BF16)
    far = part(3, [one, one])
    far = [send(far[0], ALONG_Z), send(far[1], BACK_Z)]
    here = part(0, [one, one, shape((1, 1), F32)])
    parts = [here[0], send(here[1], PARTNER_A)]
    loss = here[2]
    near = part(1, [one, one])
    parts += [send(near[1], ALONG_YZ), send(near[0], BACK_Z)]
    sums = part(2, [one, one], *far)
    parts += [send(sums[1], BACK_YZ), send(sums[0], ALONG_Z)]
    total = views * 128
    rows = views // 4
    block = pl.BlockSpec((rows, width), lambda i: (i, 0))
    grad_embed = pl.pallas_call(
        final_kernel,
        grid=(views // rows,),
        out_shape=shape((views, width), F32),
        in_specs=[SMEM] + [block] * 7,
        out_specs=block,
        compiler_params=small,
    )(inv_temp / total, embeddings, *parts)
    return (loss / total).reshape(1), grad_embed


def solution(mesh):
    in_specs = (P(("row", "col"), None), P(("row", "col")), P())
    out_specs = (P(), P(("row", "col"), None))
    return jax.shard_map(body, mesh=mesh, in_specs=in_specs, out_specs=out_specs, check_vma=False)
```

```python
import functools

import jax
import jax.numpy as jnp
from jax import lax
from jax.experimental import pallas as pl
from jax.experimental.pallas import tpu as pltpu
from jax.sharding import PartitionSpec as P

F32 = jnp.float32
BF16 = jnp.bfloat16
I32 = jnp.int32
LANES = 128
EXTRA = 8
BLOCK = 256
VMEM_LIMIT = 16 << 20
AXES = ("row", "col")
VMEM = pl.BlockSpec(memory_space=pltpu.VMEM)
SMEM = pl.BlockSpec(memory_space=pltpu.SMEM)
ANY = pl.BlockSpec(memory_space=pl.ANY)


def device_id(x, y, z, core):
    return ((x % 4) * 4 + (y % 2) * 2 + core) * 8 + (y % 4) // 2 * 4 + z % 4


def mate_a(y):
    return y ^ 1


def mate_b(y):
    return (y + 1) % 4 if y % 2 else (y - 1) % 4


def to(where):
    pairs = []
    for x in range(4):
        for y in range(4):
            for z in range(4):
                for k in range(2):
                    pairs.append((device_id(x, y, z, k), device_id(*where(x, y, z, k, 1 - 2 * k))))
    return pairs


SWAP = to(lambda x, y, z, k, g: (x, y, z, 1 - k))
ALONG_Z = to(lambda x, y, z, k, g: (x, y, z + g, k))
ALONG_X = to(lambda x, y, z, k, g: (x + g, y, z, k))
ALONG_YZ = to(lambda x, y, z, k, g: (x, mate_a(y), z + g, k))
ALONG_XY = to(lambda x, y, z, k, g: (x + g, mate_b(y), z, k))
ALONG_Y = to(lambda x, y, z, k, g: (x, mate_b(y) if k else mate_a(y), z, k))

PARTNER_A = to(lambda x, y, z, k, g: (x, mate_a(y), z, k))
PARTNER_B = to(lambda x, y, z, k, g: (x, mate_b(y), z, k))
FROM_Z = [to(lambda x, y, z, k, g, d=d: (x, y, z - d, k)) for d in (1, 2, 3)]
FROM_X = [to(lambda x, y, z, k, g, d=d: (x - d, y, z, k)) for d in (1, 2, 3)]

BACK_Z = to(lambda x, y, z, k, g: (x, y, z - g, k))
BACK_YZ = to(lambda x, y, z, k, g: (x, mate_a(y), z - g, k))

COLUMNS = [
    (0, 0, 0), (0, 0, 1), (-1, 0, 0), (-1, 0, 1), (-1, 1, 0), (-1, 1, 1), (1, 0, 1), (1, 0, 0),
    (1, 1, 1), (1, 1, 0), (2, 0, 0), (2, 1, 0), (2, 0, 1), (2, 1, 1), (0, 1, 0), (0, 1, 1),
]


def eye(n):
    return lax.broadcasted_iota(I32, (n, n), 0) == lax.broadcasted_iota(I32, (n, n), 1)


def to_column(row):
    return jnp.sum(jnp.where(eye(row.shape[1]), row, jnp.zeros_like(row)), axis=1, keepdims=True)


def to_row(column):
    return jnp.sum(jnp.where(eye(column.shape[0]), column, jnp.zeros_like(column)), axis=0, keepdims=True)


def unit_kernel(x_ref, mates_ref, out_ref):
    flat = x_ref[...].astype(F32)
    inv = lax.rsqrt(jnp.sum(flat * flat, axis=1, keepdims=True) + 1e-06)
    out_ref[0:LANES, :] = (flat * inv).astype(BF16)
    mates = mates_ref[...]
    row = jnp.concatenate([mates >> 7, mates & 127, jnp.zeros((1, out_ref.shape[1] - 2 * LANES), I32)], axis=1)
    out_ref[LANES:, :] = jnp.broadcast_to(row.astype(F32), (2 * EXTRA, row.shape[1])).astype(BF16)


def score_kernel(
    place, scale_ref, own, rz, d_a, fz, s_z, ry, s_ry, rx, d_b, s_rx, s_db, fx, s_fx,
    s_ref, b_ref, stats_ref, mates_ref, a_ref,
):
    core, y, z = place[0], place[1], place[2]
    scale = scale_ref[0]
    n, e = LANES, 2 * LANES

    def put(ref, at, src, start, rows=n):
        ref[at * n : at * n + rows, :] = src[start : start + rows, :]

    put(a_ref, 0, own, 0)
    put(a_ref, 2, rz, 0)
    put(a_ref, 3, s_z, n)
    put(a_ref, 4, s_z, 0)
    put(a_ref, 5, d_a, 0)
    put(a_ref, 6, fz, 0, e)
    for src, at in ((own, 0), (rx, 2), (d_b, 4), (s_rx, 6), (s_db, 8), (fx, 10), (s_fx, 12)):
        put(b_ref, at, src, 0, e)

    @pl.when(core == 0)
    def _():
        put(a_ref, 1, ry, 0)
        put(b_ref, 14, s_ry, n)
        put(b_ref, 15, s_ry, 0)

    @pl.when(core == 1)
    def _():
        put(a_ref, 1, s_ry, n)
        put(b_ref, 14, ry, 0, e)

    tail = lambda src: src[e : e + 2 * EXTRA, 0 : 2 * n].astype(F32)
    tails = [tail(src) for src in (own, rz, d_a, fz, s_z, ry, s_ry)]
    head = [(0, 0), (1, 0), (4, EXTRA), (4, 0), (2, 0), (3, 0), (3, EXTRA)]
    rows = [tails[p][r : r + 1] for p, r in head]
    rows.insert(1, jnp.where(core == 0, tails[5][0:1], tails[6][EXTRA : EXTRA + 1]))
    rows = jnp.concatenate(rows, axis=0).astype(I32)
    shard, lane = rows[:, 0:n], rows[:, n:]
    mate_x, mate_k, mate_z = shard >> 5, (shard >> 3) & 1, shard & 3
    mate_y = ((shard >> 2) & 1) * 2 + ((shard >> 4) & 1)
    slot = (1 - (mate_y & 1)) * 4 + mate_x + jnp.where(mate_k == core, 0, 8)
    local = jnp.zeros_like(slot)
    for t in range(16):
        local = jnp.where(slot == place[11 + t], t * n + lane, local)
    here = (mate_z == z) & ((((mate_y + 1) & 3) >> 1) == (((y + 1) & 3) >> 1))
    mates_ref[...] = jnp.where(here, local, -1)

    n_a, n_b = s_ref.shape
    wide = 512
    per = BLOCK // n

    def scores_of(step):
        a = a_ref[step * BLOCK : (step + 1) * BLOCK, :]
        peak = None
        for j in range(n_b // wide):
            b = b_ref[j * wide : (j + 1) * wide, :]
            part = lax.dot_general(a, b, (((1,), (1,)), ((), ())), preferred_element_type=F32) * scale
            if step == 0 and j == 0:
                r = lax.broadcasted_iota(I32, (BLOCK, wide), 0)
                c = lax.broadcasted_iota(I32, (BLOCK, wide), 1)
                part = jnp.where((r == c) & (r < n), -jnp.inf, part)
            s_ref[step * BLOCK : (step + 1) * BLOCK, j * wide : (j + 1) * wide] = part
            for t in range(wide // n):
                s = part[:, t * n : (t + 1) * n]
                peak = s if peak is None else jnp.maximum(peak, s)
        return jnp.max(peak, axis=1, keepdims=True)

    def stats_of(step, peaks):
        lane = lax.broadcasted_iota(I32, (n, n), 1)
        for i in range(per):
            shard = step * per + i
            rows = slice(shard * n, (shard + 1) * n)
            mates = to_column(mates_ref[shard : shard + 1, :])
            peak = peaks[i * n : (i + 1) * n]
            sums = jnp.zeros((n, n), F32)
            pos = jnp.zeros((n, n), F32)
            for t in range(n_b // n):
                s = s_ref[rows, t * n : (t + 1) * n]
                sums = sums + jnp.exp(s - peak)
                pos = pos + jnp.where(lane == mates - t * n, s, 0.0)
            values = (peak, jnp.sum(sums, axis=1, keepdims=True), jnp.sum(pos, axis=1, keepdims=True))
            for q, value in enumerate(values):
                value = to_row(value)
                stats_ref[q, pl.ds(place[3 + shard], 1), :] = value

    steps = n_a // BLOCK
    for step in range(steps):
        stats_of(step, scores_of(step))


def merge_kernel(place, g0, g1, g2, g3, lse_ref, out_ref):
    y, z = place[1], place[2]
    parts = []
    for slot in range(8):
        turn = jnp.where((y & 1) == slot // 4, 0, 1)
        step = (slot % 4 - z) & 3
        part = g0[turn]
        for d, g in ((1, g1), (2, g2), (3, g3)):
            part = jnp.where(step == d, g[turn], part)
        parts.append(part)
    peak = parts[0][0]
    for part in parts[1:]:
        peak = jnp.maximum(peak, part[0])
    total = jnp.zeros_like(peak)
    pos = jnp.zeros_like(peak)
    for part in parts:
        total = total + part[1] * jnp.exp(part[0] - peak)
        pos = pos + part[2]
    lse = peak + jnp.log(total)
    lse_ref[...] = lse
    shard = lax.broadcasted_iota(I32, lse.shape, 0)
    out_ref[0:1, :] = jnp.sum(jnp.where(shard == place[3], lse, 0.0), axis=0, keepdims=True)
    out_ref[1:2, :] = jnp.sum(lse - pos, axis=0, keepdims=True)


def grad_kernel(which, place, s_ref, b_ref, lse_ref, h0, h1, h2, h3, mates_ref, *refs):
    n = LANES
    per = BLOCK // n
    n_b = s_ref.shape[1]
    outs, d_ref = refs[per:] if which == 2 else refs, refs[-1]
    if which == 0:
        core, y, x = place[0], place[1], place[27]
        total = jnp.zeros((1, n), F32)
        for i in range(16):
            step = (i // 4 - x) & 3
            at = jnp.where((y >> 1) == i // 2 % 2, 0, 2) + jnp.where(core == i % 2, 0, 1)
            part = h0[at, 1:2, :]
            for d, h in ((1, h1), (2, h2), (3, h3)):
                part = jnp.where(step == d, h[at, 1:2, :], part)
            total = total + part
        refs[per][...] = jnp.sum(total, axis=1, keepdims=True)
    core = place[0]
    lane = lax.broadcasted_iota(I32, (n, n), 1)

    forward = jnp.where(core == 0, 1, 0)

    def other_lse(t):
        turn, twin = COLUMNS[t][1:]
        at = 2 * turn + twin
        if COLUMNS[t][0] == 0:
            return h0[at, 0:1, :]
        if COLUMNS[t][0] == 2:
            return h2[at, 0:1, :]
        ahead, behind = h1[at, 0:1, :], h3[at, 0:1, :]
        return jnp.where(forward == (1 if COLUMNS[t][0] > 0 else 0), ahead, behind)

    others = [other_lse(t) for t in range(n_b // n)]

    for i in range(per):
        shard = which * per + i
        mates = to_column(mates_ref[shard : shard + 1, :])
        mine = to_column(lse_ref[pl.ds(place[3 + shard], 1), :])
        for t in range(n_b // n):
            cols = slice(t * n, (t + 1) * n)
            s = s_ref[shard * n : (shard + 1) * n, cols]
            mate = jnp.where(lane == mates - t * n, 1.0, 0.0)
            d = (jnp.exp(s - mine) - mate) + (jnp.exp(s - others[t]) - mate)
            d_ref[i * n : (i + 1) * n, cols] = d.astype(BF16)
    out = jnp.dot(d_ref[...], b_ref[...], preferred_element_type=F32)
    for i in range(per):
        shard = out[i * n : (i + 1) * n]
        if which == 2:
            shard = shard + refs[i][...].astype(F32)
        outs[i][...] = shard.astype(BF16)


def final_kernel(scale_ref, x_ref, *refs):
    parts, out_ref = refs[:-1], refs[-1]
    flat = x_ref[...].astype(F32)
    inv = lax.rsqrt(jnp.sum(flat * flat, axis=1, keepdims=True) + 1e-06)
    unit = flat * inv
    dunit = parts[0][...].astype(F32)
    for part in parts[1:]:
        dunit = dunit + part[...].astype(F32)
    dunit = dunit * scale_ref[0]
    out_ref[...] = inv * (dunit - unit * jnp.sum(unit * dunit, axis=1, keepdims=True))


def shape(dims, dtype):
    return jax.ShapeDtypeStruct(dims, dtype)


def body(embeddings, partner, inv_temp):
    views, width = embeddings.shape
    row, col = lax.axis_index("row").astype(I32), lax.axis_index("col").astype(I32)
    x, core, z = row >> 2, row & 1, col & 3
    y = (col >> 2) * 2 + ((row >> 1) & 1)
    sign = 1 - 2 * core
    other_y = jnp.where((y & 1) == 1, y + 1, y - 1) & 3
    slot_a = lambda yy, zz: (yy & 1) * 4 + (zz & 3)
    slot_b = lambda xx, yy, same: (1 - (yy & 1)) * 4 + (xx & 3) + (0 if same else 8)
    slots_a = [
        slot_a(y, z), slot_a(y ^ 1, z), slot_a(y, z - sign), slot_a(y ^ 1, z + sign),
        slot_a(y, z + sign), slot_a(y ^ 1, z - sign), slot_a(y, z + 2), slot_a(y ^ 1, z + 2),
    ]
    slots_b = [
        slot_b(x, y, True), slot_b(x, y, False),
        slot_b(x - sign, y, True), slot_b(x - sign, y, False),
        slot_b(x - sign, other_y, True), slot_b(x - sign, other_y, False),
        slot_b(x + sign, y, False), slot_b(x + sign, y, True),
        slot_b(x + sign, other_y, False), slot_b(x + sign, other_y, True),
        slot_b(x + 2, y, True), slot_b(x + 2, other_y, True),
        slot_b(x + 2, y, False), slot_b(x + 2, other_y, False),
        slot_b(x, other_y, True), slot_b(x, other_y, False),
    ]
    place = jnp.stack([core, y, z, *slots_a, *slots_b, x]).astype(I32)
    send = lambda v, pairs: lax.ppermute(v, AXES, pairs)
    n = LANES
    params = pltpu.CompilerParams(vmem_limit_bytes=VMEM_LIMIT)
    small = pltpu.CompilerParams(vmem_limit_bytes=8 << 20)
    whole = pltpu.CompilerParams(vmem_limit_bytes=60 << 20)

    mine = pl.pallas_call(
        unit_kernel, out_shape=shape((views + 2 * EXTRA, width), BF16), in_specs=[VMEM, VMEM], out_specs=VMEM, compiler_params=whole
    )(embeddings, partner.reshape(1, views))
    twin = send(mine, SWAP)
    own = jnp.concatenate([mine[:n], twin[:n], mine[n : n + EXTRA], twin[n : n + EXTRA]], axis=0)
    d_a = send(own, ALONG_YZ)
    d_b = send(own, ALONG_XY)
    rz = send(own, ALONG_Z)
    rx = send(own, ALONG_X)
    ry = send(own, ALONG_Y)
    e = 2 * n
    fz = send(jnp.concatenate([rz[:n], d_a[:n], rz[e : e + EXTRA], d_a[e : e + EXTRA]], axis=0), ALONG_Z)
    fx = send(jnp.concatenate([rx[:n], d_b[:n]], axis=0), ALONG_X)
    s_rx, s_db, s_ry = send(rx, SWAP), send(d_b, SWAP), send(ry, SWAP)
    s_z = send(jnp.concatenate([rz[n:e], d_a[n:e], rz[e + EXTRA :], d_a[e + EXTRA :]], axis=0), SWAP)
    s_fx = send(fx, SWAP)

    n_a, n_b = 8 * views, 16 * views
    fast = lambda v: pltpu.with_memory_space_constraint(v, pltpu.VMEM)
    pieces = [fast(v) for v in (own, rz, d_a, fz, s_z, ry, s_ry, rx, d_b, s_rx, s_db, fx, s_fx)]
    scores, block_b, stats, mates = pl.pallas_call(
        score_kernel,
        out_shape=[
            pltpu.VMEM((n_a, n_b), F32),
            pltpu.VMEM((n_b, width), BF16),
            shape((3, 8, views), F32),
            shape((8, views), I32),
        ],
        in_specs=[SMEM, SMEM] + [VMEM] * 13,
        out_specs=[VMEM] * 4,
        scratch_shapes=[pltpu.VMEM((n_a, width), BF16)],
        compiler_params=params,
    )(place, inv_temp, *pieces)
    pair = jnp.stack([stats, send(stats, PARTNER_A)])
    g1, g2, g3 = (send(pair, pairs) for pairs in FROM_Z)
    lse, spread = pl.pallas_call(
        merge_kernel,
        out_shape=[shape((8, views), F32), shape((2, views), F32)],
        in_specs=[SMEM] + [VMEM] * 4,
        out_specs=[VMEM, VMEM],
        compiler_params=small,
    )(place, pair, g1, g2, g3)
    twins = jnp.stack([spread, send(spread, SWAP)])
    four = jnp.concatenate([twins, send(twins, PARTNER_B)], axis=0)
    h1, h2, h3 = (send(four, pairs) for pairs in FROM_X)
    scores, block_b = fast(scores), fast(block_b)

    def part(which, outs, *more):
        return pl.pallas_call(
            functools.partial(grad_kernel, which),
            out_shape=outs,
            in_specs=[SMEM] + [VMEM] * (8 + len(more)),
            out_specs=[VMEM] * len(outs),
            scratch_shapes=[pltpu.VMEM((BLOCK, n_b), BF16)],
            compiler_params=pltpu.CompilerParams(vmem_limit_bytes=16 << 20),
            cost_estimate=pl.CostEstimate(flops=4 * BLOCK * n_b * width, bytes_accessed=1 << 20, transcendentals=0),
        )(place, scores, block_b, lse, four, h1, h2, h3, mates, *more)

    one = shape((views, width), BF16)
    far = part(3, [one, one])
    far = [send(far[0], ALONG_Z), send(far[1], BACK_Z)]
    here = part(0, [one, one, shape((1, 1), F32)])
    parts = [here[0], send(here[1], PARTNER_A)]
    loss = here[2]
    near = part(1, [one, one])
    parts += [send(near[1], ALONG_YZ), send(near[0], BACK_Z)]
    sums = part(2, [one, one], *far)
    parts += [send(sums[1], BACK_YZ), send(sums[0], ALONG_Z)]
    total = views * 128
    rows = views // 4
    block = pl.BlockSpec((rows, width), lambda i: (i, 0))
    grad_embed = pl.pallas_call(
        final_kernel,
        grid=(views // rows,),
        out_shape=shape((views, width), F32),
        in_specs=[SMEM] + [block] * 7,
        out_specs=block,
        compiler_params=small,
    )(inv_temp / total, embeddings, *parts)
    return (loss / total).reshape(1), grad_embed


def solution(mesh):
    in_specs = (P(("row", "col"), None), P(("row", "col")), P())
    out_specs = (P(), P(("row", "col"), None))
    return jax.shard_map(body, mesh=mesh, in_specs=in_specs, out_specs=out_specs, check_vma=False)
```
